32 devices in a mesh: wide: 16 (over z, x, core), narrow: 2 (over y).
Axes of the slice: x: 2, y: 2, z: 4, core: 2. Of those that a mesh axis runs over, the one named last changes fastest.
Arguments:
- activation_cache: bfloat16 [16, 128, 8192], P('wide', None, 'narrow'), may hold values from -6 to 6
- token_ids: int32 [16, 128], P('wide'), may hold values from 0 to 127
- cotangent: bfloat16 [16, 128, 37120], P('wide', None, 'narrow'), may hold values from -6 to 6
- adapter_b: float32 [16, 16, 8192], P('wide', None, 'narrow'), may hold values from -4 to 4
- first_b: float32 [16, 16, 8192], P('wide', None, 'narrow'), may hold values from -0.3 to 0.3
- second_b: float32 [16, 16, 8192], P('wide', None, 'narrow'), may hold values from 0.0001 to 0.002
- adapter_a: float32 [16, 16, 37120], P('wide', None, 'narrow'), may hold values from -4 to 4
- first_a: float32 [16, 16, 37120], P('wide', None, 'narrow'), may hold values from -0.3 to 0.3
- second_a: float32 [16, 16, 37120], P('wide', None, 'narrow'), may hold values from 0.0001 to 0.002
- resident: bfloat16 [8192, 37120], P('narrow', 'wide'), may hold values from -6 to 6
- block_owner: int32 [16], replicated, may hold values from 0 to 15, each once
- next_rows: bfloat16 [512, 8192], P('wide', 'narrow'), may hold values from -6 to 6
Outputs:
- merged: bfloat16 [8192, 37120], P('narrow', 'wide')
- projected: bfloat16 [512, 37120], P('narrow', 'wide')
The draws below stay inside these ranges and needn't reach their ends.
Inputs may be any that keep to these rules, and one draw needn't show every extreme that they name: `block_owner`: each column block is stored at exactly one position.
All inputs are finite; a program needn't handle non-finite values.
Results may differ from the reference program's by a relative error of at most 0.0058.
Values may be sent and summed in bfloat16 or wider, within the bound.
No kernel may reach another device: no remote copies, remote signals or barrier semaphores. Data moves between devices by JAX's collectives and lax.ppermute only.
A program may use at most 128 MiB of HBM per device.

```python
import math
import jax
import jax.numpy as jnp
from jax import lax

D = 8192
FW = 37120
R = 16
WORKER_TOKENS = 128
POOL = 128
NEXT = 512
WORKER_COUNT = 16
NB = 16
FB = 2320


def set_ends(entries, stream_key, least, top_value):
    dims = entries.shape
    spot = [jax.random.randint(jax.random.fold_in(stream_key, axis), (), 0, dims[axis]) for axis in range(len(dims))]
    entries = entries.at[tuple(spot)].set(least)
    longest = dims.index(max(dims))
    spot[longest] = (spot[longest] + 1) % dims[longest]
    return entries.at[tuple(spot)].set(top_value)


def block_levels(own_key, extent, cuts, smallest, high):
    gain, own = 1.0, jax.random.fold_in(own_key, 6)
    for axis_at, blocks in cuts:
        heights = jnp.exp(jax.random.uniform(jax.random.fold_in(own, axis_at), (blocks,), jnp.float32, smallest / len(cuts), high / len(cuts)))
        gain = gain * jnp.repeat(heights, extent[axis_at] // blocks).reshape([-1 if axis == axis_at else 1 for axis in range(len(extent))])
    return gain


def noise(key, shape, deviation, most, pieces=(), kind=jnp.bfloat16):
    factor_of = block_levels(key, shape, pieces, -0.22, 0.18) if pieces else 1.0
    result = jax.random.normal(key, shape, jnp.float32) * deviation * factor_of
    return jnp.minimum(jnp.maximum(result, -most), most).astype(kind)


def setup_inputs(seed: int = 0) -> dict:
    seeds = jax.random.split(jax.random.key(seed), 13)
    activation_cache = noise(seeds[0], (WORKER_COUNT, POOL, D), 1.0, 6.0, ((0, 16), (2, 2)))
    token_ids = set_ends(jax.random.randint(seeds[1], (WORKER_COUNT, WORKER_TOKENS), 0, POOL), jax.random.fold_in(seeds[1], 1), 0, POOL - 1).astype(jnp.int32)
    cotangent = noise(seeds[2], (WORKER_COUNT, WORKER_TOKENS, FW), 1.0, 6.0, ((0, 16), (2, 2)))
    adapter_b = noise(seeds[3], (WORKER_COUNT, R, D), 0.7, 4.0, ((0, 16), (2, 2)), jnp.float32)
    first_b = noise(seeds[4], (WORKER_COUNT, R, D), 0.05, 0.3, ((0, 16), (2, 2)), jnp.float32)
    second_b = jnp.clip(jnp.exp(math.log(0.002) - 2.9957323 * jax.random.uniform(seeds[5], (WORKER_COUNT, R, D), jnp.float32) ** block_levels(seeds[5], (WORKER_COUNT, R, D), ((0, 16), (2, 2)), -0.2, 0.2)), 0.0001, 0.002)
    adapter_a = noise(seeds[6], (WORKER_COUNT, R, FW), 0.7, 4.0, ((0, 16), (2, 2)), jnp.float32)
    first_a = noise(seeds[7], (WORKER_COUNT, R, FW), 0.05, 0.3, ((0, 16), (2, 2)), jnp.float32)
    second_a = jnp.clip(jnp.exp(math.log(0.002) - 2.9957323 * jax.random.uniform(seeds[8], (WORKER_COUNT, R, FW), jnp.float32) ** block_levels(seeds[8], (WORKER_COUNT, R, FW), ((0, 16), (2, 2)), -0.2, 0.2)), 0.0001, 0.002)
    resident = noise(seeds[9], (D, FW), 1.0, 6.0, ((0, 2), (1, 16)))
    block_owner = jax.random.permutation(seeds[10], NB).astype(jnp.int32)
    next_rows = noise(seeds[11], (NEXT, D), 1.0, 6.0, ((0, 16), (1, 2)))
    return dict(activation_cache=activation_cache, token_ids=token_ids, cotangent=cotangent, adapter_b=adapter_b, first_b=first_b, second_b=second_b, adapter_a=adapter_a, first_a=first_a, second_a=second_a, resident=resident, block_owner=block_owner, next_rows=next_rows)


adapter_scale = 4.0
rate = 0.2
beta_one = 0.9
beta_two = 0.999
bias_one = 1.0 - 0.9 ** 20
bias_two = 1.0 - 0.999 ** 20
eps_adam = 1e-08

def adam_step(param, first, second, grad):
    first_new = beta_one * first + (1.0 - beta_one) * grad
    second_new = beta_two * second + (1.0 - beta_two) * grad * grad
    update = first_new / bias_one / (jnp.sqrt(second_new / bias_two) + eps_adam)
    return (param - rate * update).astype(jnp.bfloat16)

def reference(activation_cache, token_ids, cotangent, adapter_b, first_b, second_b, adapter_a, first_a, second_a, resident, block_owner, next_rows):
    inverse_root = 1.0 / math.sqrt(D)
    highest_precision = lax.Precision.HIGHEST

    def one_worker(items):
        cache, chosen, incoming_gradient, factor_b, mom_b1, mom_b2, factor_a, mom_a1, mom_a2 = items
        selected_rows = jnp.take(cache, chosen, axis=0).astype(jnp.float32)
        incoming_gradient = incoming_gradient.astype(jnp.float32)
        hidden_state = jnp.dot(selected_rows, factor_b.T, precision=highest_precision) * inverse_root
        upstream_gradient = jnp.dot(incoming_gradient, factor_a.T, precision=highest_precision)
        gradient_left = adapter_scale / WORKER_TOKENS * jnp.dot(hidden_state.T, incoming_gradient, precision=highest_precision)
        gradient_right = adapter_scale * inverse_root / WORKER_TOKENS * jnp.dot(upstream_gradient.T, selected_rows, precision=highest_precision)
        return (adam_step(factor_b, mom_b1, mom_b2, gradient_right), adam_step(factor_a, mom_a1, mom_a2, gradient_left))
    new_b, new_a = lax.map(one_worker, (activation_cache, token_ids, cotangent, adapter_b, first_b, second_b, adapter_a, first_a, second_a))
    left = new_b.reshape(WORKER_COUNT * R, D)

    def one_block(items):
        position, owner = items
        right = lax.dynamic_slice_in_dim(new_a, (owner * FB).astype(jnp.int32), FB, 2).reshape(WORKER_COUNT * R, FB)
        weight_change = lax.dot_general(left, right, (((0,), (0,)), ((), ())), preferred_element_type=jnp.float32)
        stored_weight = lax.dynamic_slice_in_dim(resident, (position * FB).astype(jnp.int32), FB, 1)
        refreshed_block = (stored_weight.astype(jnp.float32) + adapter_scale / WORKER_COUNT * weight_change).astype(jnp.bfloat16)
        block_proj = (jnp.dot(next_rows, refreshed_block, preferred_element_type=jnp.float32) * inverse_root).astype(jnp.bfloat16)
        return (refreshed_block, block_proj)
    positions = jnp.arange(NB, dtype=jnp.int32)
    blocks_new, blocks_proj = lax.map(one_block, (positions, block_owner.astype(jnp.int32)))
    merged = jnp.transpose(blocks_new, (1, 0, 2)).reshape(D, NB * FB)
    projected = jnp.transpose(blocks_proj, (1, 0, 2)).reshape(NEXT, NB * FB)
    return (merged, projected)
```

```python
import functools
import math

import jax
import jax.numpy as jnp
from jax import lax
from jax.experimental import pallas as pl
from jax.experimental.pallas import tpu as pltpu
from jax.sharding import PartitionSpec as P

adapter_scale = 4.0
rate = 0.2
beta_one = 0.9
beta_two = 0.999
bias_one = 1.0 - 0.9**20
bias_two = 1.0 - 0.999**20
eps_adam = 1e-08

F32 = jnp.float32
BF16 = jnp.bfloat16
MIB = 1024 * 1024
VMEM_LIMIT = 56 * MIB


def adam_step(param, first, second, grad):
    first_new = beta_one * first + (1.0 - beta_one) * grad
    second_new = beta_two * second + (1.0 - beta_two) * grad * grad
    root = jnp.sqrt(second_new * (1.0 / bias_two)) + eps_adam
    return (param - (rate / bias_one) * first_new / root).astype(BF16)


def plain_call(kernel, flops, moved, **kw):
    return pl.pallas_call(
        kernel,
        compiler_params=pltpu.CompilerParams(
            vmem_limit_bytes=VMEM_LIMIT,
            dimension_semantics=("arbitrary",) * len(kw.get("grid", ())),
        ),
        cost_estimate=pl.CostEstimate(flops=flops, bytes_accessed=moved, transcendentals=0),
        **kw,
    )


def in_vmem():
    return pl.BlockSpec(memory_space=pltpu.VMEM)


def anywhere():
    return pl.BlockSpec(memory_space=pl.ANY)


def split(value):
    top = value.astype(BF16)
    left = value - top.astype(F32)
    middle = left.astype(BF16)
    bottom = (left - middle.astype(F32)).astype(BF16)
    return jnp.concatenate([top, middle, bottom], axis=0)


def fold(value):
    rows = value.shape[0] // 3
    return value[:rows] + (value[rows : 2 * rows] + value[2 * rows :])


def dot_rows(value, other):
    return fold(
        lax.dot_general(split(value), other, (((1,), (1,)), ((), ())), preferred_element_type=F32)
    )


def dot_plain(parts, other):
    return fold(jnp.dot(parts, other, preferred_element_type=F32))


def column_tile(columns, most):
    count = columns // 128
    best = max(d for d in range(1, count + 1) if count % d == 0 and d * 128 <= most)
    return best * 128


def row_tile(rows, most):
    return max(d for d in range(16, most + 1, 16) if rows % d == 0)


def products(cache, factor_b, cotangent, factor_a):
    _, rank, columns = factor_a.shape
    tokens = cotangent.shape[1]
    pool, features = cache.shape[1:]
    tile = column_tile(columns, 4096)

    def kernel(cache_ref, b_ref, cot_ref, a_ref, out_ref):
        @pl.when(pl.program_id(0) == 0)
        def _():
            out_ref[:rank] = dot_rows(b_ref[...], cache_ref[...])
            out_ref[rank:] = jnp.zeros((rank, tokens), F32)

        out_ref[rank:] += dot_rows(a_ref[...], cot_ref[...])

    return plain_call(
        kernel,
        6 * rank * (tokens * columns + pool * features),
        2 * tokens * columns + 4 * rank * columns + 2 * pool * features + 4 * rank * features,
        grid=(columns // tile,),
        in_specs=[
            pl.BlockSpec((None, pool, features), lambda i: (0, 0, 0)),
            pl.BlockSpec((None, rank, features), lambda i: (0, 0, 0)),
            pl.BlockSpec((None, tokens, tile), lambda i: (0, 0, i)),
            pl.BlockSpec((None, rank, tile), lambda i: (0, 0, i)),
        ],
        out_specs=pl.BlockSpec((2 * rank, tokens), lambda i: (0, 0)),
        out_shape=jax.ShapeDtypeStruct((2 * rank, tokens), F32),
        name="products",
    )(cache, factor_b, cotangent, factor_a)


def adam(ids, own, other, cache, b_set, cotangent, a_set, block_cols, inverse_root, after):
    _, rank, columns = a_set[0].shape
    tokens = cotangent.shape[1]
    pool, features = cache.shape[1:]
    tile = column_tile(columns, 4096)
    steps = columns // tile
    blocks = columns // block_cols
    count = len(after)

    def kernel(ids_ref, own_ref, other_ref, cache_ref, b0, b1, b2, cot_ref, a0, a1, a2, *rest):
        out_b, out_a, whole, hidden = rest[count:]
        step = pl.program_id(0)

        @pl.when(step == 0)
        def _():
            sums = own_ref[...] + other_ref[...]
            chosen = lax.broadcasted_iota(jnp.int32, (pool, tokens), 0) == ids_ref[...]
            chosen = chosen.astype(F32).astype(BF16)
            hidden[...] = split(dot_plain(split(sums[:rank] * inverse_root), chosen))
            upstream = dot_rows(sums[rank:], chosen)
            grad = (adapter_scale * inverse_root / tokens) * dot_plain(
                split(upstream), cache_ref[...]
            )
            out_b[...] = adam_step(b0[...], b1[...], b2[...], grad)

        grad = (adapter_scale / tokens) * dot_plain(hidden[...], cot_ref[...])
        new = adam_step(a0[...], a1[...], a2[...], grad)
        for s in range(steps):

            @pl.when(step == s)
            def _():
                whole[:, s * tile : (s + 1) * tile] = new

        @pl.when(step == steps - 1)
        def _():
            for c in range(blocks):
                out_a[c] = whole[:, c * block_cols : (c + 1) * block_cols]

    fixed = lambda i: (0, 0, 0)
    return plain_call(
        kernel,
        6 * rank * (tokens * columns + pool * features),
        2 * tokens * columns + 14 * rank * columns + 2 * pool * features + 14 * rank * features,
        grid=(steps,),
        in_specs=[
            pl.BlockSpec((1, tokens), lambda i: (0, 0)),
            pl.BlockSpec((2 * rank, tokens), lambda i: (0, 0)),
            pl.BlockSpec((2 * rank, tokens), lambda i: (0, 0)),
            pl.BlockSpec((None, pool, features), fixed),
        ]
        + [pl.BlockSpec((None, rank, features), fixed)] * 3
        + [pl.BlockSpec((None, tokens, tile), lambda i: (0, 0, i))]
        + [pl.BlockSpec((None, rank, tile), lambda i: (0, 0, i))] * 3
        + [anywhere()] * count,
        out_specs=[
            pl.BlockSpec((rank, features), lambda i: (0, 0)),
            pl.BlockSpec((blocks, rank, block_cols), fixed),
        ],
        out_shape=[
            jax.ShapeDtypeStruct((rank, features), BF16),
            jax.ShapeDtypeStruct((blocks, rank, block_cols), BF16),
        ],
        scratch_shapes=[
            pltpu.VMEM((rank, columns), BF16),
            pltpu.VMEM((3 * rank, tokens), BF16),
        ],
        name="adam",
    )(ids, own, other, cache, *b_set, cotangent, *a_set, *after)


def across(value, wide, flip):
    return lax.ppermute(value, "wide", [(i, i ^ flip) for i in range(wide)])


def other_side(value):
    return lax.ppermute(value, "narrow", [(0, 1), (1, 0)])


def ring_pair(at, pairs):
    return jnp.where(at < pairs // 2, 2 * at, 2 * pairs - 1 - 2 * at)


def ring_place(pair, pairs):
    return jnp.where(pair % 2 == 0, pair // 2, pairs - 1 - pair // 2)


def ring_links(wide, step):
    pairs = wide // 2
    order = list(range(0, pairs, 2)) + list(range(pairs - 1, 0, -2))
    return [
        (2 * pair + core, 2 * order[(at + step) % pairs] + core)
        for at, pair in enumerate(order)
        for core in (0, 1)
    ]


def along(value, wide, step):
    return lax.ppermute(value, "wide", ring_links(wide, step))


def piece_plan(wide, rows):
    pairs = wide // 2
    plan = [(0, 0)]
    for step in range(1, pairs // 2):
        plan += [(-step, 0), (step, 0)]
    return plan + [(-(pairs // 2), 0), (pairs // 2, rows // 2)]


def early_projection(pieces, plan, whole_next, resident, wide, rows, first, last, tile, after):
    columns, depth = resident.shape
    total = wide * rows
    half = total // 2
    pairs = wide // 2
    count = len(pieces)
    gather = whole_next is None
    height = (last - first) * tile

    def kernel(*refs):
        res_ref = refs[0]
        if gather:
            piece_refs = refs[1 : 1 + count]
            own_ref, away_ref, rows_ref, sems = refs[1 + count + len(after) :]

            @pl.when(pl.program_id(0) == 0)
            def _():
                side = lax.axis_index("narrow")
                device = lax.axis_index("wide")
                at = ring_place(device // 2, pairs)
                copies = []
                for i, ref in enumerate(piece_refs):
                    distance, offset = plan[i // 2]
                    pair = ring_pair((at + distance + pairs) % pairs, pairs)
                    source = 2 * pair + (device + i) % 2
                    row = ((source // pairs + side) % 2) * half + (source % pairs) * rows + offset
                    copy = pltpu.make_async_copy(
                        ref,
                        rows_ref.at[pl.ds(pl.multiple_of(row, 16), ref.shape[0])],
                        sems.at[i],
                    )
                    copy.start()
                    copies.append(copy)
                for copy in copies:
                    copy.wait()

        else:
            rows_ref = refs[1]
            own_ref, away_ref = refs[2 + len(after) :]
        value = lax.dot_general(
            res_ref[...], rows_ref[...], (((1,), (1,)), ((), ())), preferred_element_type=F32
        )
        own_ref[...] = value[:, :half]
        away_ref[...] = value[:, half:].astype(BF16)

    out_specs = [pl.BlockSpec((tile, half), lambda i: (i, 0))] * 2
    out_shape = [
        jax.ShapeDtypeStruct((height, half), F32),
        jax.ShapeDtypeStruct((height, half), BF16),
    ]
    scratch = []
    if gather:
        out_specs.append(pl.BlockSpec((total, depth), lambda i: (0, 0)))
        out_shape.append(jax.ShapeDtypeStruct((total, depth), BF16))
        scratch = [pltpu.SemaphoreType.DMA((count,))]
        operands = list(pieces)
        specs = [anywhere()] * count
    else:
        operands = [whole_next]
        specs = [pl.BlockSpec((total, depth), lambda i: (0, 0))]
    return plain_call(
        kernel,
        2 * total * depth * height,
        2 * depth * height + 2 * total * depth + 6 * half * height,
        grid=(last - first,),
        in_specs=[pl.BlockSpec((tile, depth), lambda i: (first + i, 0))]
        + specs
        + [anywhere()] * len(after),
        out_specs=out_specs,
        out_shape=out_shape,
        scratch_shapes=scratch,
        name="early_projection",
    )(resident, *operands, *after)


def low_rank_rows(all_next, left):
    total, depth = all_next.shape
    ranks = left.shape[0]
    half = total // 2
    tile = column_tile(depth, 1024)

    def kernel(next_ref, left_ref, own_ref, away_ref):
        @pl.when(pl.program_id(0) == 0)
        def _():
            own_ref[...] = jnp.zeros_like(own_ref)
            away_ref[...] = jnp.zeros_like(away_ref)

        value = lax.dot_general(
            left_ref[...], next_ref[...], (((1,), (1,)), ((), ())), preferred_element_type=F32
        )
        own_ref[...] += value[:, :half]
        away_ref[...] += value[:, half:]

    return plain_call(
        kernel,
        2 * total * depth * ranks,
        2 * depth * (total + ranks) + 4 * total * ranks,
        grid=(depth // tile,),
        in_specs=[
            pl.BlockSpec((total, tile), lambda i: (0, i)),
            pl.BlockSpec((ranks, tile), lambda i: (0, i)),
        ],
        out_specs=[pl.BlockSpec((ranks, half), lambda i: (0, 0))] * 2,
        out_shape=[jax.ShapeDtypeStruct((ranks, half), F32)] * 2,
        name="low_rank_rows",
    )(all_next, left)


def sort_blocks(block_owner, own, other, wide):
    blocks, rank, block_cols = own.shape
    pairs = wide // 2

    def kernel(owner_ref, own_ref, other_ref, mine_ref, yours_ref):
        side = lax.axis_index("narrow")
        device = lax.axis_index("wide")
        core = device % 2
        for flip in range(pairs):
            for o, out_ref in ((0, mine_ref), (1, yours_ref)):
                block = owner_ref[2 * ((device // 2) ^ flip) + (core + o) % 2]
                here = block // blocks == side

                @pl.when(here)
                def _():
                    out_ref[flip] = own_ref[block % blocks]

                @pl.when(jnp.logical_not(here))
                def _():
                    out_ref[flip] = other_ref[block % blocks]

    shape = jax.ShapeDtypeStruct((pairs, rank, block_cols), own.dtype)
    return plain_call(
        kernel,
        0,
        8 * pairs * rank * block_cols,
        in_specs=[pl.BlockSpec(memory_space=pltpu.SMEM), in_vmem(), in_vmem()],
        out_specs=[in_vmem(), in_vmem()],
        out_shape=[shape, shape],
        name="sort_blocks",
    )(block_owner, own, other)


def merge(resident, left, pieces, scale):
    columns, depth = resident.shape
    ranks = left.shape[0]
    rank = pieces[0].shape[1]
    tile = column_tile(depth, 512)
    count = len(pieces)

    def kernel(res_ref, left_ref, *refs):
        out_ref, turned_ref, right_ref = refs[count:]

        @pl.when(pl.program_id(0) == 0)
        def _():
            device = lax.axis_index("wide")
            for flip, ref in enumerate(refs[:count]):
                for o in (0, 1):
                    worker = 2 * ((device // 2) ^ flip) + (device + o) % 2
                    right_ref[pl.ds(pl.multiple_of(worker * rank, rank), rank), :] = ref[o]
            for at in range(0, columns, 256):
                width = min(256, columns - at)
                unit = lax.broadcasted_iota(jnp.int32, (width, width), 0)
                unit = unit == lax.broadcasted_iota(jnp.int32, (width, width), 1)
                turned_ref[at : at + width] = lax.dot_general(
                    unit.astype(F32).astype(BF16),
                    right_ref[:, at : at + width],
                    (((1,), (1,)), ((), ())),
                    preferred_element_type=F32,
                ).astype(BF16)

        delta = jnp.dot(turned_ref[...], left_ref[...], preferred_element_type=F32)
        out_ref[...] = (res_ref[...].astype(F32) + scale * delta).astype(BF16)

    return plain_call(
        kernel,
        2 * depth * columns * ranks,
        4 * depth * columns + 2 * ranks * (depth + columns),
        grid=(depth // tile,),
        in_specs=[
            pl.BlockSpec((columns, tile), lambda i: (0, i)),
            pl.BlockSpec((ranks, tile), lambda i: (0, i)),
        ]
        + [pl.BlockSpec(pieces[0].shape, lambda i: (0, 0, 0))] * count,
        out_specs=[
            pl.BlockSpec((columns, tile), lambda i: (0, i)),
            pl.BlockSpec((columns, ranks), lambda i: (0, 0)),
        ],
        out_shape=[
            jax.ShapeDtypeStruct((columns, depth), BF16),
            jax.ShapeDtypeStruct((columns, ranks), BF16),
        ],
        scratch_shapes=[pltpu.VMEM((ranks, columns), BF16)],
        name="merge",
    )(resident, left, *pieces)


def finish(parts, low_own, low_other, turned, scale, inverse_root):
    ranks, half = low_own.shape
    columns = turned.shape[0]

    def kernel(own_low_ref, other_low_ref, turned_ref, *refs):
        out_ref = refs[-1]
        low = own_low_ref[...] + other_low_ref[...]
        high = low.astype(BF16)
        rest = (low - high.astype(F32)).astype(BF16)
        at = 0
        for i in range(len(parts)):
            own, other = refs[2 * i : 2 * i + 2]
            height = own.shape[0]
            right = turned_ref[at : at + height]
            shift = jnp.dot(right, high, preferred_element_type=F32) + jnp.dot(
                right, rest, preferred_element_type=F32
            )
            out_ref[at : at + height] = (
                (own[...] + other[...].astype(F32) + scale * shift) * inverse_root
            ).astype(BF16)
            at += height

    return plain_call(
        kernel,
        4 * half * ranks * columns,
        8 * half * columns + 2 * ranks * columns,
        in_specs=[in_vmem()] * (2 * len(parts) + 3),
        out_specs=in_vmem(),
        out_shape=jax.ShapeDtypeStruct((columns, half), BF16),
        name="finish",
    )(low_own, low_other, turned, *[x for part in parts for x in part])


def per_device(
    activation_cache,
    token_ids,
    cotangent,
    adapter_b,
    first_b,
    second_b,
    adapter_a,
    first_a,
    second_a,
    resident,
    block_owner,
    next_rows,
):
    inverse_root = 1.0 / math.sqrt(2 * next_rows.shape[1])
    wide = lax.axis_size("wide")
    pairs = wide // 2
    rows = next_rows.shape[0]
    resident = resident.T
    block_cols = resident.shape[0]
    scale = adapter_scale / wide
    hold = lax.optimization_barrier

    plan = piece_plan(wide, rows)
    pieces = [next_rows, across(next_rows, wide, 1)]

    def keep(piece):
        pieces.extend([piece, across(piece, wide, 1)])

    ahead, behind = along(next_rows, wide, 1), along(next_rows, wide, -1)
    own_sums = products(activation_cache, adapter_b, cotangent, adapter_a)
    other_sums = other_side(own_sums)
    ahead, behind, own_sums = hold((ahead, behind, own_sums))
    keep(ahead)
    keep(behind)
    new_b, own_blocks = adam(
        token_ids,
        own_sums,
        other_sums,
        activation_cache,
        (adapter_b, first_b, second_b),
        cotangent,
        (adapter_a, first_a, second_a),
        block_cols,
        inverse_root,
        (ahead, behind),
    )
    left = lax.all_gather(new_b, "wide", axis=0, tiled=True)
    other_blocks = other_side(own_blocks)
    for step in range(2, pairs // 2):
        ahead, behind = along(ahead, wide, 1), along(behind, wide, -1)
        keep(ahead)
        keep(behind)
    keep(along(ahead[: rows // 2], wide, 1))
    keep(along(behind[rows // 2 :], wide, -1))

    mine, yours = sort_blocks(block_owner, own_blocks, other_blocks, wide)
    handed = across(yours, wide, 1)

    tile = row_tile(block_cols, 512)
    tiles = block_cols // tile
    cut = (tiles + 1) // 2
    own_0, away_0, all_next = early_projection(
        pieces, plan, None, resident, wide, rows, 0, cut, tile, ()
    )
    got_0 = other_side(away_0)
    right = []
    for flip in range(pairs):
        piece = jnp.stack([mine[flip], handed[flip]])
        right.append(across(piece, wide, 2 * flip) if flip else piece)
    own_1, away_1 = early_projection(
        [], plan, all_next, resident, wide, rows, cut, tiles, tile, ()
    )
    got_1 = other_side(away_1)

    low_own, low_away = low_rank_rows(all_next, left)
    low_other = other_side(low_away)
    merged, turned = merge(resident, left, right, scale)
    projected = finish(
        ((own_0, got_0), (own_1, got_1)), low_own, low_other, turned, scale, inverse_root
    )
    return (merged.T, projected.T)


def any_mesh(
    activation_cache,
    token_ids,
    cotangent,
    adapter_b,
    first_b,
    second_b,
    adapter_a,
    first_a,
    second_a,
    resident,
    block_owner,
    next_rows,
):
    inverse_root = 1.0 / math.sqrt(next_rows.shape[1] * lax.axis_size("narrow"))
    highest_precision = lax.Precision.HIGHEST
    worker_group = lax.axis_size("wide")
    block_cols = resident.shape[1]
    selected_rows = jnp.take(activation_cache[0], token_ids[0], axis=0).astype(jnp.float32)
    incoming_gradient = cotangent[0].astype(jnp.float32)
    factor_b = adapter_b[0]
    factor_a = adapter_a[0]
    part_hidden = jnp.dot(selected_rows, factor_b.T, precision=highest_precision)
    part_upstream = jnp.dot(incoming_gradient, factor_a.T, precision=highest_precision)
    hidden_state, upstream_gradient = lax.psum((part_hidden, part_upstream), "narrow")
    hidden_state = hidden_state * inverse_root
    gradient_left = (
        adapter_scale
        / token_ids.shape[1]
        * jnp.dot(hidden_state.T, incoming_gradient, precision=highest_precision)
    )
    gradient_right = (
        adapter_scale
        * inverse_root
        / token_ids.shape[1]
        * jnp.dot(upstream_gradient.T, selected_rows, precision=highest_precision)
    )
    new_b = adam_step(factor_b, first_b[0], second_b[0], gradient_right)
    new_a = adam_step(factor_a, first_a[0], second_a[0], gradient_left)
    full_a = lax.all_gather(new_a, "narrow", axis=1, tiled=True)
    blocks = full_a.reshape(full_a.shape[0], worker_group, block_cols)
    ordered = jnp.take(blocks, block_owner, axis=1)
    arrived = lax.all_to_all(ordered, "wide", split_axis=1, concat_axis=0, tiled=True)
    right_rows = arrived.reshape(worker_group * full_a.shape[0], block_cols)
    weight_change = lax.dot_general(
        lax.all_gather(new_b, "wide", axis=0, tiled=True),
        right_rows,
        (((0,), (0,)), ((), ())),
        preferred_element_type=jnp.float32,
    )
    merged = (resident.astype(jnp.float32) + adapter_scale / worker_group * weight_change).astype(
        jnp.bfloat16
    )
    all_next = lax.all_gather(next_rows, "wide", axis=0, tiled=True)
    summed = lax.psum_scatter(
        jnp.dot(all_next, merged, preferred_element_type=jnp.float32),
        "narrow",
        scatter_dimension=0,
        tiled=True,
    )
    projected = (summed * inverse_root).astype(jnp.bfloat16)
    return (merged, projected)


def solution(mesh):
    paired = mesh.shape["narrow"] == 2 and mesh.shape["wide"] == 16
    return jax.shard_map(
        per_device if paired else any_mesh,
        mesh=mesh,
        in_specs=(
            P("wide", None, "narrow"),
            P("wide", None),
            P("wide", None, "narrow"),
            P("wide", None, "narrow"),
            P("wide", None, "narrow"),
            P("wide", None, "narrow"),
            P("wide", None, "narrow"),
            P("wide", None, "narrow"),
            P("wide", None, "narrow"),
            P("narrow", "wide"),
            P(),
            P("wide", "narrow"),
        ),
        out_specs=(P("narrow", "wide"), P("narrow", "wide")),
        check_vma=False,
    )
```

```python
import functools
import math

import jax
import jax.numpy as jnp
from jax import lax
from jax.experimental import pallas as pl
from jax.experimental.pallas import tpu as pltpu
from jax.sharding import PartitionSpec as P

adapter_scale = 4.0
rate = 0.2
beta_one = 0.9
beta_two = 0.999
bias_one = 1.0 - 0.9**20
bias_two = 1.0 - 0.999**20
eps_adam = 1e-08

F32 = jnp.float32
BF16 = jnp.bfloat16
MIB = 1024 * 1024


def adam_step(param, first, second, grad):
    first_new = beta_one * first + (1.0 - beta_one) * grad
    second_new = beta_two * second + (1.0 - beta_two) * grad * grad
    root = jnp.sqrt(second_new * (1.0 / bias_two)) + eps_adam
    return (param - (rate / bias_one) * first_new / root).astype(BF16)


def plain_call(kernel, flops, moved, limit, weight=1, **kw):
    return pl.pallas_call(
        kernel,
        compiler_params=pltpu.CompilerParams(vmem_limit_bytes=limit * MIB),
        cost_estimate=pl.CostEstimate(flops=weight * flops, bytes_accessed=moved, transcendentals=0),
        **kw,
    )


def in_vmem():
    return pl.BlockSpec(memory_space=pltpu.VMEM)


def split(value):
    top = value.astype(BF16)
    left = value - top.astype(F32)
    middle = left.astype(BF16)
    bottom = (left - middle.astype(F32)).astype(BF16)
    return jnp.concatenate([top, middle, bottom], axis=0)


def fold(value):
    rows = value.shape[0] // 3
    return value[:rows] + (value[rows : 2 * rows] + value[2 * rows :])


def dot_rows(value, other):
    return fold(
        lax.dot_general(
            value, split(other), (((1,), (1,)), ((), ())), preferred_element_type=F32
        ).T
    )


def dot_plain(parts, other):
    return fold(jnp.dot(parts, other, preferred_element_type=F32))


def column_tile(columns, most):
    count = columns // 128
    best = max(d for d in range(1, count + 1) if count % d == 0 and d * 128 <= most)
    return best * 128


def row_tile(rows, most):
    return max(d for d in range(16, most + 1, 16) if rows % d == 0)


def products(cache, factor_b, cotangent, factor_a):
    rank, columns = factor_a.shape
    tokens = cotangent.shape[0]
    pool, features = cache.shape

    tile = column_tile(columns, 4096)

    def kernel(cache_ref, b_ref, cot_ref, a_ref, out_ref):
        value = dot_rows(cot_ref[...], a_ref[...])

        @pl.when(pl.program_id(0) == 0)
        def _():
            out_ref[:rank] = dot_rows(cache_ref[...], b_ref[...])
            out_ref[rank:] = value

        @pl.when(pl.program_id(0) > 0)
        def _():
            out_ref[rank:] += value

    fixed = lambda i: (0, 0)
    return plain_call(
        kernel,
        6 * rank * (tokens * columns + pool * features),
        2 * tokens * columns + 4 * rank * columns + 2 * pool * features + 4 * rank * features,
        8,
        512,
        grid=(columns // tile,),
        in_specs=[
            pl.BlockSpec((pool, features), fixed),
            pl.BlockSpec((rank, features), fixed),
            pl.BlockSpec((tokens, tile), lambda i: (0, i)),
            pl.BlockSpec((rank, tile), lambda i: (0, i)),
        ],
        out_specs=pl.BlockSpec((2 * rank, tokens), fixed),
        out_shape=jax.ShapeDtypeStruct((2 * rank, tokens), F32),
        name="products",
    )(cache, factor_b, cotangent, factor_a)


def adam(ids, own, other, cache, b_set, cotangent, a_set, block_cols, inverse_root, early):
    rank, columns = a_set[0].shape
    tokens = cotangent.shape[0]
    pool, features = cache.shape
    tile = column_tile(columns, 4096)
    blocks = columns // block_cols

    def kernel(ids_ref, own_ref, other_ref, cache_ref, b0, b1, b2, cot_ref, a0, a1, a2, *rest):
        out_b, out_a, whole = rest[1:]
        sums = own_ref[...] + other_ref[...]
        chosen = lax.broadcasted_iota(jnp.int32, (pool, tokens), 0) == ids_ref[...]
        chosen = chosen.astype(F32).astype(BF16)
        hidden = split(dot_plain(split(sums[:rank] * inverse_root), chosen))
        upstream = split(
            fold(
                lax.dot_general(
                    split(sums[rank:]), chosen, (((1,), (1,)), ((), ())), preferred_element_type=F32
                )
            )
        )
        grad = (adapter_scale * inverse_root / tokens) * dot_plain(upstream, cache_ref[...])
        out_b[...] = adam_step(b0[...], b1[...], b2[...], grad)
        for at in range(0, columns, tile):
            part = slice(at, at + tile)
            grad = (adapter_scale / tokens) * dot_plain(hidden, cot_ref[:, part])
            whole[:, part] = adam_step(a0[:, part], a1[:, part], a2[:, part], grad)
        for c in range(blocks):
            out_a[c] = whole[:, c * block_cols : (c + 1) * block_cols]

    return plain_call(
        kernel,
        6 * rank * (tokens * columns + pool * features),
        2 * tokens * columns + 14 * rank * columns + 2 * pool * features + 14 * rank * features,
        10,
        64,
        in_specs=[in_vmem()] * 12,
        out_specs=[in_vmem()] * 2,
        out_shape=[
            jax.ShapeDtypeStruct((rank, features), BF16),
            jax.ShapeDtypeStruct((blocks, rank, block_cols), BF16),
        ],
        scratch_shapes=[pltpu.VMEM((rank, columns), BF16)],
        name="adam",
    )(ids, own, other, cache, *b_set, cotangent, *a_set, early)


def across(value, wide, flip):
    return lax.ppermute(value, "wide", [(i, i ^ flip) for i in range(wide)])


def other_side(value):
    return lax.ppermute(value, "narrow", [(0, 1), (1, 0)])


def ring_pair(at, pairs):
    return jnp.where(at < pairs // 2, 2 * at, 2 * pairs - 1 - 2 * at)


def ring_place(pair, pairs):
    return jnp.where(pair % 2 == 0, pair // 2, pairs - 1 - pair // 2)


def ring_links(wide, step):
    pairs = wide // 2
    order = list(range(0, pairs, 2)) + list(range(pairs - 1, 0, -2))
    return [
        (2 * pair + core, 2 * order[(at + step) % pairs] + core)
        for at, pair in enumerate(order)
        for core in (0, 1)
    ]


def along(value, wide, step):
    return lax.ppermute(value, "wide", ring_links(wide, step))


def piece_plan(wide):
    pairs = wide // 2
    plan = [0]
    for step in range(1, pairs // 2):
        plan += [-step, step]
    return plan + [pairs // 2]


def order_rows(pieces, plan, wide, by_side):
    rows, depth = pieces[0].shape
    total = wide * rows
    half = total // 2
    pairs = wide // 2

    def kernel(*refs):
        side = lax.axis_index("narrow") if by_side else 0
        device = lax.axis_index("wide")
        at = ring_place(device // 2, pairs)
        for i, ref in enumerate(refs[:-1]):
            pair = ring_pair((at + plan[i // 2] + pairs) % pairs, pairs)
            source = 2 * pair + (device + i) % 2
            row = ((source // pairs + side) % 2) * half + (source % pairs) * rows
            refs[-1][pl.ds(pl.multiple_of(row, 16), ref.shape[0]), :] = ref[...]

    return plain_call(
        kernel,
        0,
        4 * total * depth,
        4,
        in_specs=[in_vmem()] * len(pieces),
        out_specs=in_vmem(),
        out_shape=jax.ShapeDtypeStruct((total, depth), BF16),
        name="order_rows",
    )(*pieces)


def early_projection(resident, all_next, first, last, away):
    columns, depth = resident.shape
    half = all_next.shape[0] // 2
    kind = BF16 if away else F32

    def kernel(res_ref, rows_ref, out_ref):
        out_ref[...] = lax.dot_general(
            res_ref[first:last],
            rows_ref[away * half : (away + 1) * half],
            (((1,), (1,)), ((), ())),
            preferred_element_type=F32,
        ).astype(kind)

    return plain_call(
        kernel,
        2 * half * depth * (last - first),
        2 * depth * (last - first + half) + 4 * half * (last - first),
        16,
        in_specs=[in_vmem()] * 2,
        out_specs=in_vmem(),
        out_shape=jax.ShapeDtypeStruct((last - first, half), kind),
        name="early_projection",
    )(resident, all_next)


def low_rank_rows(all_next, left):
    total, depth = all_next.shape
    ranks = left.shape[0]
    half = total // 2

    def kernel(next_ref, left_ref, own_ref, away_ref):
        value = lax.dot_general(
            left_ref[...], next_ref[...], (((1,), (1,)), ((), ())), preferred_element_type=F32
        )
        own_ref[...] = value[:, :half]
        away_ref[...] = value[:, half:]

    return plain_call(
        kernel,
        2 * total * depth * ranks,
        2 * depth * (total + ranks) + 4 * total * ranks,
        4,
        64,
        in_specs=[in_vmem()] * 2,
        out_specs=[in_vmem()] * 2,
        out_shape=[jax.ShapeDtypeStruct((ranks, half), F32)] * 2,
        name="low_rank_rows",
    )(all_next, left)


def sort_blocks(block_owner, own, other, wide):
    blocks, rank, block_cols = own.shape
    pairs = wide // 2

    def kernel(owner_ref, own_ref, other_ref, mine_ref, yours_ref):
        side = lax.axis_index("narrow")
        device = lax.axis_index("wide")
        core = device % 2
        for flip in range(pairs):
            for o, out_ref in ((0, mine_ref), (1, yours_ref)):
                block = owner_ref[2 * ((device // 2) ^ flip) + (core + o) % 2]
                here = block // blocks == side

                @pl.when(here)
                def _():
                    out_ref[flip] = own_ref[block % blocks]

                @pl.when(jnp.logical_not(here))
                def _():
                    out_ref[flip] = other_ref[block % blocks]

    shape = jax.ShapeDtypeStruct((pairs, rank, block_cols), own.dtype)
    return plain_call(
        kernel,
        0,
        8 * pairs * rank * block_cols,
        4,
        in_specs=[pl.BlockSpec(memory_space=pltpu.SMEM), in_vmem(), in_vmem()],
        out_specs=[in_vmem(), in_vmem()],
        out_shape=[shape, shape],
        name="sort_blocks",
    )(block_owner, own, other)


def pair_blocks(mine, handed):
    pairs, rank, block_cols = mine.shape

    def kernel(mine_ref, handed_ref, *out_refs):
        for flip, ref in enumerate(out_refs):
            ref[0] = mine_ref[flip]
            ref[1] = handed_ref[flip]

    return plain_call(
        kernel,
        0,
        8 * pairs * rank * block_cols,
        4,
        in_specs=[in_vmem()] * 2,
        out_specs=[in_vmem()] * pairs,
        out_shape=[jax.ShapeDtypeStruct((2, rank, block_cols), mine.dtype)] * pairs,
        name="pair_blocks",
    )(mine, handed)


def merge(resident, left, pieces, scale):
    columns, depth = resident.shape
    ranks = left.shape[0]
    rank = pieces[0].shape[1]
    tile = row_tile(columns, 512)
    count = len(pieces)

    def kernel(res_ref, left_ref, *refs):
        out_ref, turned_ref, right_ref = refs[count:]
        step = pl.program_id(0)

        @pl.when(step == 0)
        def _():
            device = lax.axis_index("wide")
            for flip, ref in enumerate(refs[:count]):
                for o in (0, 1):
                    worker = 2 * ((device // 2) ^ flip) + (device + o) % 2
                    right_ref[pl.ds(pl.multiple_of(worker * rank, rank), rank), :] = ref[o]
            for at in range(0, columns, 256):
                width = min(256, columns - at)
                unit = lax.broadcasted_iota(jnp.int32, (width, width), 0)
                unit = unit == lax.broadcasted_iota(jnp.int32, (width, width), 1)
                turned_ref[at : at + width] = (
                    scale
                    * lax.dot_general(
                        unit.astype(F32).astype(BF16),
                        right_ref[:, at : at + width],
                        (((1,), (1,)), ((), ())),
                        preferred_element_type=F32,
                    )
                ).astype(BF16)

        rows = pl.ds(pl.multiple_of(step * tile, 16), tile)
        for at in range(0, depth, depth // 4):
            cols = slice(at, at + depth // 4)
            delta = jnp.dot(turned_ref[rows, :], left_ref[:, cols], preferred_element_type=F32)
            out_ref[:, cols] = (res_ref[rows, cols].astype(F32) + delta).astype(BF16)

    return plain_call(
        kernel,
        2 * depth * columns * ranks,
        4 * depth * columns + 2 * ranks * (depth + columns),
        16,
        grid=(columns // tile,),
        in_specs=[in_vmem()] * (2 + count),
        out_specs=[pl.BlockSpec((tile, depth), lambda i: (i, 0)), in_vmem()],
        out_shape=[
            jax.ShapeDtypeStruct((columns, depth), BF16),
            jax.ShapeDtypeStruct((columns, ranks), BF16),
        ],
        scratch_shapes=[pltpu.VMEM((ranks, columns), BF16)],
        name="merge",
    )(resident, left, *pieces)


def finish(own_part, others, low_own, low_other, turned, inverse_root):
    ranks, half = low_own.shape
    columns = turned.shape[0]

    def kernel(own_low_ref, other_low_ref, turned_ref, own_ref, *refs):
        out_ref = refs[-1]
        low = own_low_ref[...] + other_low_ref[...]
        high = low.astype(BF16)
        rest = (low - high.astype(F32)).astype(BF16)
        at = 0
        for other in refs[:-1]:
            part = slice(at, at + other.shape[0])
            shift = jnp.dot(turned_ref[part], high, preferred_element_type=F32) + jnp.dot(
                turned_ref[part], rest, preferred_element_type=F32
            )
            out_ref[part] = (
                (own_ref[part] + other[...].astype(F32) + shift) * inverse_root
            ).astype(BF16)
            at += other.shape[0]

    return plain_call(
        kernel,
        4 * half * ranks * columns,
        8 * half * columns + 2 * ranks * columns,
        8,
        in_specs=[in_vmem()] * (4 + len(others)),
        out_specs=in_vmem(),
        out_shape=jax.ShapeDtypeStruct((columns, half), BF16),
        name="finish",
    )(low_own, low_other, turned, own_part, *others)


def per_device(
    activation_cache,
    token_ids,
    cotangent,
    adapter_b,
    first_b,
    second_b,
    adapter_a,
    first_a,
    second_a,
    resident,
    block_owner,
    next_rows,
):
    inverse_root = 1.0 / math.sqrt(2 * next_rows.shape[1])
    wide = lax.axis_size("wide")
    pairs = wide // 2
    resident = resident.T
    block_cols = resident.shape[0]
    cache, incoming = activation_cache[0], cotangent[0]
    scale = adapter_scale / wide
    hold = lax.optimization_barrier

    plan = piece_plan(wide)
    pieces = [next_rows, across(next_rows, wide, 1)]

    def keep(pieces, *blocks):
        for block in blocks:
            pieces.extend([block, across(block, wide, 1)])

    def both_ways(ahead, behind):
        return along(ahead, wide, 1), along(behind, wide, -1)

    step_1 = both_ways(next_rows, next_rows)
    own_sums = products(cache, adapter_b[0], incoming, adapter_a[0])
    step_1, own_sums = hold((step_1, own_sums))
    keep(pieces, *step_1)
    other_sums = other_side(own_sums)
    step_2 = both_ways(*step_1)
    step_2, other_sums = hold((step_2, other_sums))
    keep(pieces, *step_2)
    new_b, own_blocks = adam(
        token_ids,
        own_sums,
        other_sums,
        cache,
        (adapter_b[0], first_b[0], second_b[0]),
        incoming,
        (adapter_a[0], first_a[0], second_a[0]),
        block_cols,
        inverse_root,
        resident,
    )
    left_pieces = [new_b, across(new_b, wide, 1)]
    other_blocks = other_side(own_blocks)
    step_3 = both_ways(*step_2)
    left_1 = both_ways(new_b, new_b)
    step_3, left_1 = hold((step_3, left_1))
    keep(pieces, *step_3)
    keep(left_pieces, *left_1)
    step_4 = along(step_3[0], wide, 1)
    left_2 = both_ways(*left_1)
    step_4, left_2, other_blocks = hold((step_4, left_2, other_blocks))
    keep(pieces, step_4)
    keep(left_pieces, *left_2)
    left_3 = both_ways(*left_2)
    keep(left_pieces, *left_3)
    keep(left_pieces, along(left_3[0], wide, 1))
    all_next = order_rows(pieces, plan, wide, True)
    left = order_rows(left_pieces, plan, wide, False)

    mine, yours = sort_blocks(block_owner, own_blocks, other_blocks, wide)
    handed = across(yours, wide, 1)
    right = list(pair_blocks(mine, handed))
    for flip in range(1, pairs):
        right[flip] = across(right[flip], wide, 2 * flip)

    cut = -(-block_cols // 32) * 16
    got_0 = other_side(early_projection(resident, all_next, 0, cut, 1))
    got_1 = other_side(early_projection(resident, all_next, cut, block_cols, 1))
    all_next, right[1], right[2], right[3] = hold(
        (all_next, right[1], right[2], right[3])
    )
    own_part = early_projection(resident, all_next, 0, block_cols, 0)
    low_own, low_away = low_rank_rows(all_next, left)
    low_other = other_side(low_away)
    merged, turned = merge(resident, left, right, scale)
    projected = finish(own_part, (got_0, got_1), low_own, low_other, turned, inverse_root)
    return (merged.T, projected.T)


def any_mesh(
    activation_cache,
    token_ids,
    cotangent,
    adapter_b,
    first_b,
    second_b,
    adapter_a,
    first_a,
    second_a,
    resident,
    block_owner,
    next_rows,
):
    inverse_root = 1.0 / math.sqrt(next_rows.shape[1] * lax.axis_size("narrow"))
    highest_precision = lax.Precision.HIGHEST
    worker_group = lax.axis_size("wide")
    block_cols = resident.shape[1]
    selected_rows = jnp.take(activation_cache[0], token_ids[0], axis=0).astype(jnp.float32)
    incoming_gradient = cotangent[0].astype(jnp.float32)
    factor_b = adapter_b[0]
    factor_a = adapter_a[0]
    part_hidden = jnp.dot(selected_rows, factor_b.T, precision=highest_precision)
    part_upstream = jnp.dot(incoming_gradient, factor_a.T, precision=highest_precision)
    hidden_state, upstream_gradient = lax.psum((part_hidden, part_upstream), "narrow")
    hidden_state = hidden_state * inverse_root
    gradient_left = (
        adapter_scale
        / token_ids.shape[1]
        * jnp.dot(hidden_state.T, incoming_gradient, precision=highest_precision)
    )
    gradient_right = (
        adapter_scale
        * inverse_root
        / token_ids.shape[1]
        * jnp.dot(upstream_gradient.T, selected_rows, precision=highest_precision)
    )
    new_b = adam_step(factor_b, first_b[0], second_b[0], gradient_right)
    new_a = adam_step(factor_a, first_a[0], second_a[0], gradient_left)
    full_a = lax.all_gather(new_a, "narrow", axis=1, tiled=True)
    blocks = full_a.reshape(full_a.shape[0], worker_group, block_cols)
    ordered = jnp.take(blocks, block_owner, axis=1)
    arrived = lax.all_to_all(ordered, "wide", split_axis=1, concat_axis=0, tiled=True)
    right_rows = arrived.reshape(worker_group * full_a.shape[0], block_cols)
    weight_change = lax.dot_general(
        lax.all_gather(new_b, "wide", axis=0, tiled=True),
        right_rows,
        (((0,), (0,)), ((), ())),
        preferred_element_type=jnp.float32,
    )
    merged = (resident.astype(jnp.float32) + adapter_scale / worker_group * weight_change).astype(
        jnp.bfloat16
    )
    all_next = lax.all_gather(next_rows, "wide", axis=0, tiled=True)
    summed = lax.psum_scatter(
        jnp.dot(all_next, merged, preferred_element_type=jnp.float32),
        "narrow",
        scatter_dimension=0,
        tiled=True,
    )
    projected = (summed * inverse_root).astype(jnp.bfloat16)
    return (merged, projected)


def solution(mesh):
    paired = mesh.shape["narrow"] == 2 and mesh.shape["wide"] == 16
    return jax.shard_map(
        per_device if paired else any_mesh,
        mesh=mesh,
        in_specs=(
            P("wide", None, "narrow"),
            P("wide", None),
            P("wide", None, "narrow"),
            P("wide", None, "narrow"),
            P("wide", None, "narrow"),
            P("wide", None, "narrow"),
            P("wide", None, "narrow"),
            P("wide", None, "narrow"),
            P("wide", None, "narrow"),
            P("narrow", "wide"),
            P(),
            P("wide", "narrow"),
        ),
        out_specs=(P("narrow", "wide"), P("narrow", "wide")),
        check_vma=False,
    )
```

```python
import functools
import math

import jax
import jax.numpy as jnp
from jax import lax
from jax.experimental import pallas as pl
from jax.experimental.pallas import tpu as pltpu
from jax.sharding import PartitionSpec as P

adapter_scale = 4.0
rate = 0.2
beta_one = 0.9
beta_two = 0.999
bias_one = 1.0 - 0.9**20
bias_two = 1.0 - 0.999**20
eps_adam = 1e-08

F32 = jnp.float32
BF16 = jnp.bfloat16
MIB = 1024 * 1024


def adam_step(param, first, second, grad):
    first_new = beta_one * first + (1.0 - beta_one) * grad
    second_new = beta_two * second + (1.0 - beta_two) * grad * grad
    root = jnp.sqrt(second_new * (1.0 / bias_two)) + eps_adam
    return (param - (rate / bias_one) * first_new / root).astype(BF16)


def plain_call(kernel, flops, moved, limit, weight=1, **kw):
    return pl.pallas_call(
        kernel,
        compiler_params=pltpu.CompilerParams(vmem_limit_bytes=limit * MIB),
        cost_estimate=pl.CostEstimate(flops=weight * flops, bytes_accessed=moved, transcendentals=0),
        **kw,
    )


def anywhere():
    return pl.BlockSpec(memory_space=pl.ANY)


def in_vmem():
    return pl.BlockSpec(memory_space=pltpu.VMEM)


def split(value):
    top = value.astype(BF16)
    left = value - top.astype(F32)
    middle = left.astype(BF16)
    bottom = (left - middle.astype(F32)).astype(BF16)
    return jnp.concatenate([top, middle, bottom], axis=0)


def fold(value):
    rows = value.shape[0] // 3
    return value[:rows] + (value[rows : 2 * rows] + value[2 * rows :])


def dot_rows(value, other):
    return fold(
        lax.dot_general(
            value, split(other), (((1,), (1,)), ((), ())), preferred_element_type=F32
        ).T
    )


def dot_plain(parts, other):
    return fold(jnp.dot(parts, other, preferred_element_type=F32))


def column_tile(columns, most):
    count = columns // 128
    best = max(d for d in range(1, count + 1) if count % d == 0 and d * 128 <= most)
    return best * 128


def row_tile(rows, most):
    return max(d for d in range(16, most + 1, 16) if rows % d == 0)


def opening():
    def kernel(out_ref):
        out_ref[...] = jnp.zeros_like(out_ref)

    return plain_call(
        kernel,
        10**11,
        0,
        4,
        out_specs=in_vmem(),
        out_shape=jax.ShapeDtypeStruct((8, 128), F32),
        name="opening",
    )()


def products(cache, factor_b, cotangent, factor_a, after):
    rank, columns = factor_a.shape
    tokens = cotangent.shape[0]
    pool, features = cache.shape

    tile = column_tile(columns, 4096)

    def kernel(cache_ref, b_ref, cot_ref, a_ref, _, out_ref):
        value = dot_rows(cot_ref[...], a_ref[...])

        @pl.when(pl.program_id(0) == 0)
        def _():
            out_ref[:rank] = dot_rows(cache_ref[...], b_ref[...])
            out_ref[rank:] = value

        @pl.when(pl.program_id(0) > 0)
        def _():
            out_ref[rank:] += value

    fixed = lambda i: (0, 0)
    return plain_call(
        kernel,
        6 * rank * (tokens * columns + pool * features),
        2 * tokens * columns + 4 * rank * columns + 2 * pool * features + 4 * rank * features,
        8,
        512,
        grid=(columns // tile,),
        in_specs=[
            pl.BlockSpec((pool, features), fixed),
            pl.BlockSpec((rank, features), fixed),
            pl.BlockSpec((tokens, tile), lambda i: (0, i)),
            pl.BlockSpec((rank, tile), lambda i: (0, i)),
            anywhere(),
        ],
        out_specs=pl.BlockSpec((2 * rank, tokens), fixed),
        out_shape=jax.ShapeDtypeStruct((2 * rank, tokens), F32),
        name="products",
    )(cache, factor_b, cotangent, factor_a, after)


def adam(ids, own, other, cache, b_set, cotangent, a_set, block_cols, inverse_root, early):
    rank, columns = a_set[0].shape
    tokens = cotangent.shape[0]
    pool, features = cache.shape
    tile = column_tile(columns, 4096)
    blocks = columns // block_cols

    def kernel(ids_ref, own_ref, other_ref, cache_ref, b0, b1, b2, cot_ref, a0, a1, a2, *rest):
        out_b, out_a, whole = rest[1:]
        sums = own_ref[...] + other_ref[...]
        chosen = lax.broadcasted_iota(jnp.int32, (pool, tokens), 0) == ids_ref[...]
        chosen = chosen.astype(F32).astype(BF16)
        hidden = split(dot_plain(split(sums[:rank] * inverse_root), chosen))
        upstream = split(
            fold(
                lax.dot_general(
                    split(sums[rank:]), chosen, (((1,), (1,)), ((), ())), preferred_element_type=F32
                )
            )
        )
        grad = (adapter_scale * inverse_root / tokens) * dot_plain(upstream, cache_ref[...])
        out_b[...] = adam_step(b0[...], b1[...], b2[...], grad)
        for at in range(0, columns, tile):
            part = slice(at, at + tile)
            grad = (adapter_scale / tokens) * dot_plain(hidden, cot_ref[:, part])
            whole[:, part] = adam_step(a0[:, part], a1[:, part], a2[:, part], grad)
        for c in range(blocks):
            out_a[c] = whole[:, c * block_cols : (c + 1) * block_cols]

    return plain_call(
        kernel,
        6 * rank * (tokens * columns + pool * features),
        2 * tokens * columns + 14 * rank * columns + 2 * pool * features + 14 * rank * features,
        10,
        64,
        in_specs=[in_vmem()] * 12,
        out_specs=[in_vmem()] * 2,
        out_shape=[
            jax.ShapeDtypeStruct((rank, features), BF16),
            jax.ShapeDtypeStruct((blocks, rank, block_cols), BF16),
        ],
        scratch_shapes=[pltpu.VMEM((rank, columns), BF16)],
        name="adam",
    )(ids, own, other, cache, *b_set, cotangent, *a_set, early)


def across(value, wide, flip):
    return lax.ppermute(value, "wide", [(i, i ^ flip) for i in range(wide)])


def other_side(value):
    return lax.ppermute(value, "narrow", [(0, 1), (1, 0)])


def ring_pair(at, pairs):
    return jnp.where(at < pairs // 2, 2 * at, 2 * pairs - 1 - 2 * at)


def ring_place(pair, pairs):
    return jnp.where(pair % 2 == 0, pair // 2, pairs - 1 - pair // 2)


def ring_links(wide, step):
    pairs = wide // 2
    order = list(range(0, pairs, 2)) + list(range(pairs - 1, 0, -2))
    return [
        (2 * pair + core, 2 * order[(at + step) % pairs] + core)
        for at, pair in enumerate(order)
        for core in (0, 1)
    ]


def along(value, wide, step):
    return lax.ppermute(value, "wide", ring_links(wide, step))


def piece_plan(wide):
    pairs = wide // 2
    plan = [0]
    for step in range(1, pairs // 2):
        plan += [-step, step]
    return plan + [pairs // 2]


def order_rows(pieces, plan, wide, by_side):
    rows, depth = pieces[0].shape
    total = wide * rows
    half = total // 2
    pairs = wide // 2

    def kernel(*refs):
        side = lax.axis_index("narrow") if by_side else 0
        device = lax.axis_index("wide")
        at = ring_place(device // 2, pairs)
        for i, ref in enumerate(refs[:-1]):
            pair = ring_pair((at + plan[i // 2] + pairs) % pairs, pairs)
            source = 2 * pair + (device + i) % 2
            row = ((source // pairs + side) % 2) * half + (source % pairs) * rows
            refs[-1][pl.ds(pl.multiple_of(row, 16), ref.shape[0]), :] = ref[...]

    return plain_call(
        kernel,
        0,
        4 * total * depth,
        4,
        in_specs=[in_vmem()] * len(pieces),
        out_specs=in_vmem(),
        out_shape=jax.ShapeDtypeStruct((total, depth), BF16),
        name="order_rows",
    )(*pieces)


def early_projection(resident, all_next, first, last, away):
    columns, depth = resident.shape
    half = all_next.shape[0] // 2
    kind = BF16 if away else F32

    def kernel(res_ref, rows_ref, out_ref):
        out_ref[...] = lax.dot_general(
            res_ref[first:last],
            rows_ref[away * half : (away + 1) * half],
            (((1,), (1,)), ((), ())),
            preferred_element_type=F32,
        ).astype(kind)

    return plain_call(
        kernel,
        2 * half * depth * (last - first),
        2 * depth * (last - first + half) + 4 * half * (last - first),
        16,
        in_specs=[in_vmem()] * 2,
        out_specs=in_vmem(),
        out_shape=jax.ShapeDtypeStruct((last - first, half), kind),
        name="early_projection",
    )(resident, all_next)


def low_rank_rows(all_next, left):
    total, depth = all_next.shape
    ranks = left.shape[0]
    half = total // 2

    def kernel(next_ref, left_ref, own_ref, away_ref):
        value = lax.dot_general(
            left_ref[...], next_ref[...], (((1,), (1,)), ((), ())), preferred_element_type=F32
        )
        own_ref[...] = value[:, :half]
        away_ref[...] = value[:, half:]

    return plain_call(
        kernel,
        2 * total * depth * ranks,
        2 * depth * (total + ranks) + 4 * total * ranks,
        4,
        64,
        in_specs=[in_vmem()] * 2,
        out_specs=[in_vmem()] * 2,
        out_shape=[jax.ShapeDtypeStruct((ranks, half), F32)] * 2,
        name="low_rank_rows",
    )(all_next, left)


def sort_blocks(block_owner, own, other, wide):
    blocks, rank, block_cols = own.shape
    pairs = wide // 2

    def kernel(owner_ref, own_ref, other_ref, mine_ref, yours_ref):
        side = lax.axis_index("narrow")
        device = lax.axis_index("wide")
        core = device % 2
        for flip in range(pairs):
            for o, out_ref in ((0, mine_ref), (1, yours_ref)):
                block = owner_ref[2 * ((device // 2) ^ flip) + (core + o) % 2]
                here = block // blocks == side

                @pl.when(here)
                def _():
                    out_ref[flip] = own_ref[block % blocks]

                @pl.when(jnp.logical_not(here))
                def _():
                    out_ref[flip] = other_ref[block % blocks]

    shape = jax.ShapeDtypeStruct((pairs, rank, block_cols), own.dtype)
    return plain_call(
        kernel,
        0,
        8 * pairs * rank * block_cols,
        4,
        in_specs=[pl.BlockSpec(memory_space=pltpu.SMEM), in_vmem(), in_vmem()],
        out_specs=[in_vmem(), in_vmem()],
        out_shape=[shape, shape],
        name="sort_blocks",
    )(block_owner, own, other)


def pair_blocks(mine, handed):
    pairs, rank, block_cols = mine.shape

    def kernel(mine_ref, handed_ref, *out_refs):
        for flip, ref in enumerate(out_refs):
            ref[0] = mine_ref[flip]
            ref[1] = handed_ref[flip]

    return plain_call(
        kernel,
        0,
        8 * pairs * rank * block_cols,
        4,
        in_specs=[in_vmem()] * 2,
        out_specs=[in_vmem()] * pairs,
        out_shape=[jax.ShapeDtypeStruct((2, rank, block_cols), mine.dtype)] * pairs,
        name="pair_blocks",
    )(mine, handed)


def merge(resident, left, pieces, order, scale):
    columns, depth = resident.shape
    ranks = left.shape[0]
    rank = pieces[0].shape[1]
    tile = row_tile(columns, 512)
    count = len(pieces)

    def kernel(res_ref, left_ref, *refs):
        out_ref, turned_ref, right_ref = refs[count:]
        step = pl.program_id(0)

        @pl.when(step == 0)
        def _():
            device = lax.axis_index("wide")
            for flip, ref in zip(order, refs):
                for o in (0, 1):
                    worker = 2 * ((device // 2) ^ flip) + (device + o) % 2
                    right_ref[pl.ds(pl.multiple_of(worker * rank, rank), rank), :] = ref[o]
            for at in range(0, columns, 256):
                width = min(256, columns - at)
                unit = lax.broadcasted_iota(jnp.int32, (width, width), 0)
                unit = unit == lax.broadcasted_iota(jnp.int32, (width, width), 1)
                turned_ref[at : at + width] = (
                    scale
                    * lax.dot_general(
                        unit.astype(F32).astype(BF16),
                        right_ref[:, at : at + width],
                        (((1,), (1,)), ((), ())),
                        preferred_element_type=F32,
                    )
                ).astype(BF16)

        rows = pl.ds(pl.multiple_of(step * tile, 16), tile)
        for at in range(0, depth, depth // 4):
            cols = slice(at, at + depth // 4)
            delta = jnp.dot(turned_ref[rows, :], left_ref[:, cols], preferred_element_type=F32)
            out_ref[:, cols] = (res_ref[rows, cols].astype(F32) + delta).astype(BF16)

    return plain_call(
        kernel,
        2 * depth * columns * ranks,
        4 * depth * columns + 2 * ranks * (depth + columns),
        16,
        grid=(columns // tile,),
        in_specs=[in_vmem()] * (2 + count),
        out_specs=[pl.BlockSpec((tile, depth), lambda i: (i, 0)), in_vmem()],
        out_shape=[
            jax.ShapeDtypeStruct((columns, depth), BF16),
            jax.ShapeDtypeStruct((columns, ranks), BF16),
        ],
        scratch_shapes=[pltpu.VMEM((ranks, columns), BF16)],
        name="merge",
    )(resident, left, *[pieces[flip] for flip in order])


def finish(own_part, others, low_own, low_other, turned, inverse_root):
    ranks, half = low_own.shape
    columns = turned.shape[0]

    def kernel(own_low_ref, other_low_ref, turned_ref, own_ref, *refs):
        out_ref = refs[-1]
        low = own_low_ref[...] + other_low_ref[...]
        high = low.astype(BF16)
        rest = (low - high.astype(F32)).astype(BF16)
        at = 0
        for other in refs[:-1]:
            part = slice(at, at + other.shape[0])
            shift = jnp.dot(turned_ref[part], high, preferred_element_type=F32) + jnp.dot(
                turned_ref[part], rest, preferred_element_type=F32
            )
            out_ref[part] = (
                (own_ref[part] + other[...].astype(F32) + shift) * inverse_root
            ).astype(BF16)
            at += other.shape[0]

    return plain_call(
        kernel,
        4 * half * ranks * columns,
        8 * half * columns + 2 * ranks * columns,
        8,
        in_specs=[in_vmem()] * (4 + len(others)),
        out_specs=in_vmem(),
        out_shape=jax.ShapeDtypeStruct((columns, half), BF16),
        name="finish",
    )(low_own, low_other, turned, own_part, *others)


def per_device(
    activation_cache,
    token_ids,
    cotangent,
    adapter_b,
    first_b,
    second_b,
    adapter_a,
    first_a,
    second_a,
    resident,
    block_owner,
    next_rows,
):
    inverse_root = 1.0 / math.sqrt(2 * next_rows.shape[1])
    wide = lax.axis_size("wide")
    pairs = wide // 2
    resident = resident.T
    block_cols = resident.shape[0]
    cache, incoming = activation_cache[0], cotangent[0]
    scale = adapter_scale / wide
    hold = lax.optimization_barrier

    plan = piece_plan(wide)
    pieces = [next_rows, across(next_rows, wide, 1)]

    def keep(pieces, *blocks):
        for block in blocks:
            pieces.extend([block, across(block, wide, 1)])

    def both_ways(ahead, behind):
        return along(ahead, wide, 1), along(behind, wide, -1)

    step_1 = both_ways(next_rows, next_rows)
    own_sums = products(cache, adapter_b[0], incoming, adapter_a[0], opening())
    step_1, own_sums = hold((step_1, own_sums))
    keep(pieces, *step_1)
    other_sums = other_side(own_sums)
    step_2 = both_ways(*step_1)

    keep(pieces, *step_2)
    new_b, own_blocks = adam(
        token_ids,
        own_sums,
        other_sums,
        cache,
        (adapter_b[0], first_b[0], second_b[0]),
        incoming,
        (adapter_a[0], first_a[0], second_a[0]),
        block_cols,
        inverse_root,
        resident,
    )
    left_pieces = [new_b, across(new_b, wide, 1)]
    other_blocks = other_side(own_blocks)
    step_3 = both_ways(*step_2)
    left_1 = both_ways(new_b, new_b)
    step_3, left_1 = hold((step_3, left_1))
    keep(pieces, *step_3)
    keep(left_pieces, *left_1)
    step_4 = along(step_3[0], wide, 1)
    left_2 = both_ways(*left_1)
    step_4, left_2, other_blocks = hold((step_4, left_2, other_blocks))
    keep(pieces, step_4)
    keep(left_pieces, *left_2)
    left_3 = both_ways(*left_2)
    keep(left_pieces, *left_3)
    keep(left_pieces, along(left_3[0], wide, 1))
    all_next = order_rows(pieces, plan, wide, True)
    left = order_rows(left_pieces, plan, wide, False)

    mine, yours = sort_blocks(block_owner, own_blocks, other_blocks, wide)
    handed = across(yours, wide, 1)
    right = list(pair_blocks(mine, handed))
    for flip in range(1, pairs):
        right[flip] = across(right[flip], wide, 2 * flip)

    cut = -(-block_cols // 32) * 16
    got_0 = other_side(early_projection(resident, all_next, 0, cut, 1))
    got_1 = other_side(early_projection(resident, all_next, cut, block_cols, 1))
    own_part = early_projection(resident, all_next, 0, block_cols, 0)
    low_own, low_away = low_rank_rows(all_next, left)
    order = (0,1,2,3,4,5,6,7)
    low_other = other_side(low_away)
    merged, turned = merge(resident, left, right, order, scale)
    projected = finish(own_part, (got_0, got_1), low_own, low_other, turned, inverse_root)
    return (merged.T, projected.T)


def any_mesh(
    activation_cache,
    token_ids,
    cotangent,
    adapter_b,
    first_b,
    second_b,
    adapter_a,
    first_a,
    second_a,
    resident,
    block_owner,
    next_rows,
):
    inverse_root = 1.0 / math.sqrt(next_rows.shape[1] * lax.axis_size("narrow"))
    highest_precision = lax.Precision.HIGHEST
    worker_group = lax.axis_size("wide")
    block_cols = resident.shape[1]
    selected_rows = jnp.take(activation_cache[0], token_ids[0], axis=0).astype(jnp.float32)
    incoming_gradient = cotangent[0].astype(jnp.float32)
    factor_b = adapter_b[0]
    factor_a = adapter_a[0]
    part_hidden = jnp.dot(selected_rows, factor_b.T, precision=highest_precision)
    part_upstream = jnp.dot(incoming_gradient, factor_a.T, precision=highest_precision)
    hidden_state, upstream_gradient = lax.psum((part_hidden, part_upstream), "narrow")
    hidden_state = hidden_state * inverse_root
    gradient_left = (
        adapter_scale
        / token_ids.shape[1]
        * jnp.dot(hidden_state.T, incoming_gradient, precision=highest_precision)
    )
    gradient_right = (
        adapter_scale
        * inverse_root
        / token_ids.shape[1]
        * jnp.dot(upstream_gradient.T, selected_rows, precision=highest_precision)
    )
    new_b = adam_step(factor_b, first_b[0], second_b[0], gradient_right)
    new_a = adam_step(factor_a, first_a[0], second_a[0], gradient_left)
    full_a = lax.all_gather(new_a, "narrow", axis=1, tiled=True)
    blocks = full_a.reshape(full_a.shape[0], worker_group, block_cols)
    ordered = jnp.take(blocks, block_owner, axis=1)
    arrived = lax.all_to_all(ordered, "wide", split_axis=1, concat_axis=0, tiled=True)
    right_rows = arrived.reshape(worker_group * full_a.shape[0], block_cols)
    weight_change = lax.dot_general(
        lax.all_gather(new_b, "wide", axis=0, tiled=True),
        right_rows,
        (((0,), (0,)), ((), ())),
        preferred_element_type=jnp.float32,
    )
    merged = (resident.astype(jnp.float32) + adapter_scale / worker_group * weight_change).astype(
        jnp.bfloat16
    )
    all_next = lax.all_gather(next_rows, "wide", axis=0, tiled=True)
    summed = lax.psum_scatter(
        jnp.dot(all_next, merged, preferred_element_type=jnp.float32),
        "narrow",
        scatter_dimension=0,
        tiled=True,
    )
    projected = (summed * inverse_root).astype(jnp.bfloat16)
    return (merged, projected)


def solution(mesh):
    paired = mesh.shape["narrow"] == 2 and mesh.shape["wide"] == 16
    return jax.shard_map(
        per_device if paired else any_mesh,
        mesh=mesh,
        in_specs=(
            P("wide", None, "narrow"),
            P("wide", None),
            P("wide", None, "narrow"),
            P("wide", None, "narrow"),
            P("wide", None, "narrow"),
            P("wide", None, "narrow"),
            P("wide", None, "narrow"),
            P("wide", None, "narrow"),
            P("wide", None, "narrow"),
            P("narrow", "wide"),
            P(),
            P("wide", "narrow"),
        ),
        out_specs=(P("narrow", "wide"), P("narrow", "wide")),
        check_vma=False,
    )
```

```python
import functools
import math

import jax
import jax.numpy as jnp
from jax import lax
from jax.experimental import pallas as pl
from jax.experimental.pallas import tpu as pltpu
from jax.sharding import PartitionSpec as P

adapter_scale = 4.0
rate = 0.2
beta_one = 0.9
beta_two = 0.999
bias_one = 1.0 - 0.9**20
bias_two = 1.0 - 0.999**20
eps_adam = 1e-08

F32 = jnp.float32
BF16 = jnp.bfloat16
MIB = 1024 * 1024


def adam_step(param, first, second, grad):
    first_new = beta_one * first + (1.0 - beta_one) * grad
    second_new = beta_two * second + (1.0 - beta_two) * grad * grad
    root = jnp.sqrt(second_new * (1.0 / bias_two)) + eps_adam
    return (param - (rate / bias_one) * first_new / root).astype(BF16)


def plain_call(kernel, flops, moved, limit, weight=1, **kw):
    return pl.pallas_call(
        kernel,
        compiler_params=pltpu.CompilerParams(vmem_limit_bytes=limit * MIB),
        cost_estimate=pl.CostEstimate(flops=weight * flops, bytes_accessed=moved, transcendentals=0),
        **kw,
    )


def anywhere():
    return pl.BlockSpec(memory_space=pl.ANY)


def in_vmem():
    return pl.BlockSpec(memory_space=pltpu.VMEM)


def split(value):
    top = value.astype(BF16)
    left = value - top.astype(F32)
    middle = left.astype(BF16)
    bottom = (left - middle.astype(F32)).astype(BF16)
    return jnp.concatenate([top, middle, bottom], axis=0)


def fold(value):
    rows = value.shape[0] // 3
    return value[:rows] + (value[rows : 2 * rows] + value[2 * rows :])


def dot_rows(value, other):
    return fold(
        lax.dot_general(
            value, split(other), (((1,), (1,)), ((), ())), preferred_element_type=F32
        ).T
    )


def dot_plain(parts, other):
    return fold(jnp.dot(parts, other, preferred_element_type=F32))


def column_tile(columns, most):
    count = columns // 128
    best = max(d for d in range(1, count + 1) if count % d == 0 and d * 128 <= most)
    return best * 128


def row_tile(rows, most):
    return max(d for d in range(16, most + 1, 16) if rows % d == 0)


def opening():
    def kernel(out_ref):
        out_ref[...] = jnp.zeros_like(out_ref)

    return plain_call(
        kernel,
        10**11,
        0,
        4,
        out_specs=in_vmem(),
        out_shape=jax.ShapeDtypeStruct((8, 128), F32),
        name="opening",
    )()


def products(cache, factor_b, cotangent, factor_a, after):
    rank, columns = factor_a.shape
    tokens = cotangent.shape[0]
    pool, features = cache.shape

    tile = column_tile(columns, 4096)

    def kernel(cache_ref, b_ref, cot_ref, a_ref, _, out_ref):
        value = dot_rows(cot_ref[...], a_ref[...])

        @pl.when(pl.program_id(0) == 0)
        def _():
            out_ref[:rank] = dot_rows(cache_ref[...], b_ref[...])
            out_ref[rank:] = value

        @pl.when(pl.program_id(0) > 0)
        def _():
            out_ref[rank:] += value

    fixed = lambda i: (0, 0)
    return plain_call(
        kernel,
        6 * rank * (tokens * columns + pool * features),
        2 * tokens * columns + 4 * rank * columns + 2 * pool * features + 4 * rank * features,
        8,
        512,
        grid=(columns // tile,),
        in_specs=[
            pl.BlockSpec((pool, features), fixed),
            pl.BlockSpec((rank, features), fixed),
            pl.BlockSpec((tokens, tile), lambda i: (0, i)),
            pl.BlockSpec((rank, tile), lambda i: (0, i)),
            anywhere(),
        ],
        out_specs=pl.BlockSpec((2 * rank, tokens), fixed),
        out_shape=jax.ShapeDtypeStruct((2 * rank, tokens), F32),
        name="products",
    )(cache, factor_b, cotangent, factor_a, after)


def adam(ids, own, other, cache, b_set, cotangent, a_set, block_cols, inverse_root, early):
    rank, columns = a_set[0].shape
    tokens = cotangent.shape[0]
    pool, features = cache.shape
    tile = column_tile(columns, 4096)
    blocks = columns // block_cols

    def kernel(ids_ref, own_ref, other_ref, cache_ref, b0, b1, b2, cot_ref, a0, a1, a2, *rest):
        out_b, out_a, whole = rest[1:]
        sums = own_ref[...] + other_ref[...]
        chosen = lax.broadcasted_iota(jnp.int32, (pool, tokens), 0) == ids_ref[...]
        chosen = chosen.astype(F32).astype(BF16)
        hidden = split(dot_plain(split(sums[:rank] * inverse_root), chosen))
        upstream = split(
            fold(
                lax.dot_general(
                    split(sums[rank:]), chosen, (((1,), (1,)), ((), ())), preferred_element_type=F32
                )
            )
        )
        grad = (adapter_scale * inverse_root / tokens) * dot_plain(upstream, cache_ref[...])
        out_b[...] = adam_step(b0[...], b1[...], b2[...], grad)
        for at in range(0, columns, tile):
            part = slice(at, at + tile)
            grad = (adapter_scale / tokens) * dot_plain(hidden, cot_ref[:, part])
            whole[:, part] = adam_step(a0[:, part], a1[:, part], a2[:, part], grad)
        for c in range(blocks):
            out_a[c] = whole[:, c * block_cols : (c + 1) * block_cols]

    return plain_call(
        kernel,
        6 * rank * (tokens * columns + pool * features),
        2 * tokens * columns + 14 * rank * columns + 2 * pool * features + 14 * rank * features,
        10,
        64,
        in_specs=[in_vmem()] * 12,
        out_specs=[in_vmem()] * 2,
        out_shape=[
            jax.ShapeDtypeStruct((rank, features), BF16),
            jax.ShapeDtypeStruct((blocks, rank, block_cols), BF16),
        ],
        scratch_shapes=[pltpu.VMEM((rank, columns), BF16)],
        name="adam",
    )(ids, own, other, cache, *b_set, cotangent, *a_set, early)


def across(value, wide, flip):
    return lax.ppermute(value, "wide", [(i, i ^ flip) for i in range(wide)])


def other_side(value):
    return lax.ppermute(value, "narrow", [(0, 1), (1, 0)])


def ring_pair(at, pairs):
    return jnp.where(at < pairs // 2, 2 * at, 2 * pairs - 1 - 2 * at)


def ring_place(pair, pairs):
    return jnp.where(pair % 2 == 0, pair // 2, pairs - 1 - pair // 2)


def ring_links(wide, step):
    pairs = wide // 2
    order = list(range(0, pairs, 2)) + list(range(pairs - 1, 0, -2))
    return [
        (2 * pair + core, 2 * order[(at + step) % pairs] + core)
        for at, pair in enumerate(order)
        for core in (0, 1)
    ]


def along(value, wide, step):
    return lax.ppermute(value, "wide", ring_links(wide, step))


def piece_plan(wide):
    pairs = wide // 2
    plan = [0]
    for step in range(1, pairs // 2):
        plan += [-step, step]
    return plan + [pairs // 2]


def order_rows(pieces, plan, wide, by_side):
    rows, depth = pieces[0].shape
    total = wide * rows
    half = total // 2
    pairs = wide // 2

    def kernel(*refs):
        side = lax.axis_index("narrow") if by_side else 0
        device = lax.axis_index("wide")
        at = ring_place(device // 2, pairs)
        for i, ref in enumerate(refs[:-1]):
            pair = ring_pair((at + plan[i // 2] + pairs) % pairs, pairs)
            source = 2 * pair + (device + i) % 2
            row = ((source // pairs + side) % 2) * half + (source % pairs) * rows
            refs[-1][pl.ds(pl.multiple_of(row, 16), ref.shape[0]), :] = ref[...]

    return plain_call(
        kernel,
        0,
        4 * total * depth,
        4,
        in_specs=[in_vmem()] * len(pieces),
        out_specs=in_vmem(),
        out_shape=jax.ShapeDtypeStruct((total, depth), BF16),
        name="order_rows",
    )(*pieces)


def early_projection(resident, all_next, first, last, away):
    columns, depth = resident.shape
    half = all_next.shape[0] // 2
    kind = BF16 if away else F32

    def kernel(res_ref, rows_ref, out_ref):
        out_ref[...] = lax.dot_general(
            res_ref[first:last],
            rows_ref[away * half : (away + 1) * half],
            (((1,), (1,)), ((), ())),
            preferred_element_type=F32,
        ).astype(kind)

    return plain_call(
        kernel,
        2 * half * depth * (last - first),
        2 * depth * (last - first + half) + 4 * half * (last - first),
        16,
        in_specs=[in_vmem()] * 2,
        out_specs=in_vmem(),
        out_shape=jax.ShapeDtypeStruct((last - first, half), kind),
        name="early_projection",
    )(resident, all_next)


def low_rank_rows(all_next, left):
    total, depth = all_next.shape
    ranks = left.shape[0]
    half = total // 2

    def kernel(next_ref, left_ref, own_ref, away_ref):
        value = lax.dot_general(
            left_ref[...], next_ref[...], (((1,), (1,)), ((), ())), preferred_element_type=F32
        )
        own_ref[...] = value[:, :half]
        away_ref[...] = value[:, half:]

    return plain_call(
        kernel,
        2 * total * depth * ranks,
        2 * depth * (total + ranks) + 4 * total * ranks,
        4,
        64,
        in_specs=[in_vmem()] * 2,
        out_specs=[in_vmem()] * 2,
        out_shape=[jax.ShapeDtypeStruct((ranks, half), F32)] * 2,
        name="low_rank_rows",
    )(all_next, left)


def sort_blocks(block_owner, own, other, wide):
    blocks, rank, block_cols = own.shape
    pairs = wide // 2

    def kernel(owner_ref, own_ref, other_ref, mine_ref, yours_ref):
        side = lax.axis_index("narrow")
        device = lax.axis_index("wide")
        core = device % 2
        for flip in range(pairs):
            for o, out_ref in ((0, mine_ref), (1, yours_ref)):
                block = owner_ref[2 * ((device // 2) ^ flip) + (core + o) % 2]
                here = block // blocks == side

                @pl.when(here)
                def _():
                    out_ref[flip] = own_ref[block % blocks]

                @pl.when(jnp.logical_not(here))
                def _():
                    out_ref[flip] = other_ref[block % blocks]

    shape = jax.ShapeDtypeStruct((pairs, rank, block_cols), own.dtype)
    return plain_call(
        kernel,
        0,
        8 * pairs * rank * block_cols,
        4,
        in_specs=[pl.BlockSpec(memory_space=pltpu.SMEM), in_vmem(), in_vmem()],
        out_specs=[in_vmem(), in_vmem()],
        out_shape=[shape, shape],
        name="sort_blocks",
    )(block_owner, own, other)


def pair_blocks(mine, handed):
    pairs, rank, block_cols = mine.shape

    def kernel(mine_ref, handed_ref, *out_refs):
        for flip, ref in enumerate(out_refs):
            ref[0] = mine_ref[flip]
            ref[1] = handed_ref[flip]

    return plain_call(
        kernel,
        0,
        8 * pairs * rank * block_cols,
        4,
        in_specs=[in_vmem()] * 2,
        out_specs=[in_vmem()] * pairs,
        out_shape=[jax.ShapeDtypeStruct((2, rank, block_cols), mine.dtype)] * pairs,
        name="pair_blocks",
    )(mine, handed)


def merge(resident, left, pieces, order, scale):
    columns, depth = resident.shape
    ranks = left.shape[0]
    rank = pieces[0].shape[1]
    tile = row_tile(columns, 512)
    count = len(pieces)

    def kernel(res_ref, left_ref, *refs):
        out_ref, turned_ref, right_ref = refs[count:]
        step = pl.program_id(0)

        @pl.when(step == 0)
        def _():
            device = lax.axis_index("wide")
            for flip, ref in zip(order, refs):
                for o in (0, 1):
                    worker = 2 * ((device // 2) ^ flip) + (device + o) % 2
                    right_ref[pl.ds(pl.multiple_of(worker * rank, rank), rank), :] = ref[o]

        for at in range(0, columns, 256):

            @pl.when(step == at // tile)
            def _():
                width = min(256, columns - at)
                unit = lax.broadcasted_iota(jnp.int32, (width, width), 0)
                unit = unit == lax.broadcasted_iota(jnp.int32, (width, width), 1)
                turned_ref[at : at + width] = (
                    scale
                    * lax.dot_general(
                        unit.astype(F32).astype(BF16),
                        right_ref[:, at : at + width],
                        (((1,), (1,)), ((), ())),
                        preferred_element_type=F32,
                    )
                ).astype(BF16)

        rows = pl.ds(pl.multiple_of(step * tile, 16), tile)
        for at in range(0, depth, depth // 4):
            cols = slice(at, at + depth // 4)
            delta = jnp.dot(turned_ref[rows, :], left_ref[:, cols], preferred_element_type=F32)
            out_ref[:, cols] = (res_ref[rows, cols].astype(F32) + delta).astype(BF16)

    return plain_call(
        kernel,
        2 * depth * columns * ranks,
        4 * depth * columns + 2 * ranks * (depth + columns),
        16,
        grid=(columns // tile,),
        in_specs=[in_vmem()] * (2 + count),
        out_specs=[pl.BlockSpec((tile, depth), lambda i: (i, 0)), in_vmem()],
        out_shape=[
            jax.ShapeDtypeStruct((columns, depth), BF16),
            jax.ShapeDtypeStruct((columns, ranks), BF16),
        ],
        scratch_shapes=[pltpu.VMEM((ranks, columns), BF16)],
        name="merge",
    )(resident, left, *[pieces[flip] for flip in order])


def finish(own_part, others, low_own, low_other, turned, inverse_root):
    ranks, half = low_own.shape
    columns = turned.shape[0]

    def kernel(own_low_ref, other_low_ref, turned_ref, own_ref, *refs):
        out_ref = refs[-1]
        low = own_low_ref[...] + other_low_ref[...]
        high = low.astype(BF16)
        rest = (low - high.astype(F32)).astype(BF16)
        at = 0
        for other in refs[:-1]:
            part = slice(at, at + other.shape[0])
            shift = jnp.dot(turned_ref[part], high, preferred_element_type=F32) + jnp.dot(
                turned_ref[part], rest, preferred_element_type=F32
            )
            out_ref[part] = (
                (own_ref[part] + other[...].astype(F32) + shift) * inverse_root
            ).astype(BF16)
            at += other.shape[0]

    return plain_call(
        kernel,
        4 * half * ranks * columns,
        8 * half * columns + 2 * ranks * columns,
        8,
        in_specs=[in_vmem()] * (4 + len(others)),
        out_specs=in_vmem(),
        out_shape=jax.ShapeDtypeStruct((columns, half), BF16),
        name="finish",
    )(low_own, low_other, turned, own_part, *others)


def per_device(
    activation_cache,
    token_ids,
    cotangent,
    adapter_b,
    first_b,
    second_b,
    adapter_a,
    first_a,
    second_a,
    resident,
    block_owner,
    next_rows,
):
    inverse_root = 1.0 / math.sqrt(2 * next_rows.shape[1])
    wide = lax.axis_size("wide")
    pairs = wide // 2
    resident = resident.T
    block_cols = resident.shape[0]
    cache, incoming = activation_cache[0], cotangent[0]
    scale = adapter_scale / wide
    hold = lax.optimization_barrier

    plan = piece_plan(wide)
    pieces = [next_rows, across(next_rows, wide, 1)]

    def keep(pieces, *blocks):
        for block in blocks:
            pieces.extend([block, across(block, wide, 1)])

    def both_ways(ahead, behind):
        return along(ahead, wide, 1), along(behind, wide, -1)

    step_1 = both_ways(next_rows, next_rows)
    own_sums = products(cache, adapter_b[0], incoming, adapter_a[0], opening())
    step_1, own_sums = hold((step_1, own_sums))
    keep(pieces, *step_1)
    other_sums = other_side(own_sums)
    step_2 = both_ways(*step_1)

    keep(pieces, *step_2)
    new_b, own_blocks = adam(
        token_ids,
        own_sums,
        other_sums,
        cache,
        (adapter_b[0], first_b[0], second_b[0]),
        incoming,
        (adapter_a[0], first_a[0], second_a[0]),
        block_cols,
        inverse_root,
        resident,
    )
    left_pieces = [new_b, across(new_b, wide, 1)]
    other_blocks = other_side(own_blocks)
    step_3 = both_ways(*step_2)
    left_1 = both_ways(new_b, new_b)
    step_3, left_1 = hold((step_3, left_1))
    keep(pieces, *step_3)
    keep(left_pieces, *left_1)
    step_4 = along(step_3[0], wide, 1)
    left_2 = both_ways(*left_1)
    step_4, left_2, other_blocks = hold((step_4, left_2, other_blocks))
    keep(pieces, step_4)
    keep(left_pieces, *left_2)
    left_3 = both_ways(*left_2)
    keep(left_pieces, *left_3)
    keep(left_pieces, along(left_3[0], wide, 1))
    all_next = order_rows(pieces, plan, wide, True)
    left = order_rows(left_pieces, plan, wide, False)

    mine, yours = sort_blocks(block_owner, own_blocks, other_blocks, wide)
    handed = across(yours, wide, 1)
    right = list(pair_blocks(mine, handed))
    for flip in range(1, pairs):
        right[flip] = across(right[flip], wide, 2 * flip)

    cut = -(-block_cols // 32) * 16
    got_0 = other_side(early_projection(resident, all_next, 0, cut, 1))
    got_1 = other_side(early_projection(resident, all_next, cut, block_cols, 1))
    own_part = early_projection(resident, all_next, 0, block_cols, 0)
    low_own, low_away = low_rank_rows(all_next, left)
    order = (0,1,2,3,4,5,6,7)
    low_other = other_side(low_away)
    merged, turned = merge(resident, left, right, order, scale)
    projected = finish(own_part, (got_0, got_1), low_own, low_other, turned, inverse_root)
    return (merged.T, projected.T)


def any_mesh(
    activation_cache,
    token_ids,
    cotangent,
    adapter_b,
    first_b,
    second_b,
    adapter_a,
    first_a,
    second_a,
    resident,
    block_owner,
    next_rows,
):
    inverse_root = 1.0 / math.sqrt(next_rows.shape[1] * lax.axis_size("narrow"))
    highest_precision = lax.Precision.HIGHEST
    worker_group = lax.axis_size("wide")
    block_cols = resident.shape[1]
    selected_rows = jnp.take(activation_cache[0], token_ids[0], axis=0).astype(jnp.float32)
    incoming_gradient = cotangent[0].astype(jnp.float32)
    factor_b = adapter_b[0]
    factor_a = adapter_a[0]
    part_hidden = jnp.dot(selected_rows, factor_b.T, precision=highest_precision)
    part_upstream = jnp.dot(incoming_gradient, factor_a.T, precision=highest_precision)
    hidden_state, upstream_gradient = lax.psum((part_hidden, part_upstream), "narrow")
    hidden_state = hidden_state * inverse_root
    gradient_left = (
        adapter_scale
        / token_ids.shape[1]
        * jnp.dot(hidden_state.T, incoming_gradient, precision=highest_precision)
    )
    gradient_right = (
        adapter_scale
        * inverse_root
        / token_ids.shape[1]
        * jnp.dot(upstream_gradient.T, selected_rows, precision=highest_precision)
    )
    new_b = adam_step(factor_b, first_b[0], second_b[0], gradient_right)
    new_a = adam_step(factor_a, first_a[0], second_a[0], gradient_left)
    full_a = lax.all_gather(new_a, "narrow", axis=1, tiled=True)
    blocks = full_a.reshape(full_a.shape[0], worker_group, block_cols)
    ordered = jnp.take(blocks, block_owner, axis=1)
    arrived = lax.all_to_all(ordered, "wide", split_axis=1, concat_axis=0, tiled=True)
    right_rows = arrived.reshape(worker_group * full_a.shape[0], block_cols)
    weight_change = lax.dot_general(
        lax.all_gather(new_b, "wide", axis=0, tiled=True),
        right_rows,
        (((0,), (0,)), ((), ())),
        preferred_element_type=jnp.float32,
    )
    merged = (resident.astype(jnp.float32) + adapter_scale / worker_group * weight_change).astype(
        jnp.bfloat16
    )
    all_next = lax.all_gather(next_rows, "wide", axis=0, tiled=True)
    summed = lax.psum_scatter(
        jnp.dot(all_next, merged, preferred_element_type=jnp.float32),
        "narrow",
        scatter_dimension=0,
        tiled=True,
    )
    projected = (summed * inverse_root).astype(jnp.bfloat16)
    return (merged, projected)


def solution(mesh):
    paired = mesh.shape["narrow"] == 2 and mesh.shape["wide"] == 16
    return jax.shard_map(
        per_device if paired else any_mesh,
        mesh=mesh,
        in_specs=(
            P("wide", None, "narrow"),
            P("wide", None),
            P("wide", None, "narrow"),
            P("wide", None, "narrow"),
            P("wide", None, "narrow"),
            P("wide", None, "narrow"),
            P("wide", None, "narrow"),
            P("wide", None, "narrow"),
            P("wide", None, "narrow"),
            P("narrow", "wide"),
            P(),
            P("wide", "narrow"),
        ),
        out_specs=(P("narrow", "wide"), P("narrow", "wide")),
        check_vma=False,
    )
```
